32 devices in a mesh: neuron: 4 (over x, core), box: 4 (over z), spec: 2 (over y).
Axes of the slice: x: 2, y: 2, z: 4, core: 2. Of those that a mesh axis runs over, the one named last changes fastest.
Arguments:
- coeff: bfloat16 [96, 8, 8192], P('box', 'spec', 'neuron'), may hold values from -6 to 6
- weight: bfloat16 [8192, 8192], P('neuron', 'spec'), may hold values from -0.09375 to 0.09375
- upper_bound: float32 [96, 8192], P('box', 'neuron'), may hold values from 0.2 to 6, as said below
- lower_depth: float32 [96, 8192], P('box', 'neuron'), may hold values from 0.2 to 6, as said below
- slopes: float32 [96, 8192], P('box', 'neuron'), may hold values from 0 to 1
- state: int32 [96, 8192], P('box', 'neuron'), may hold values from 0 to 2
- adjoint: bfloat16 [96, 8, 8192], P('box', 'spec', 'neuron'), may hold values from -6 to 6
Outputs:
- new_coeff: bfloat16 [96, 8, 8192], P('box', 'spec', 'neuron')
- offset: float32 [96, 8], P('box', 'spec')
- slope_grad: float32 [96, 8192], P('box', 'neuron')
- coeff_grad: bfloat16 [96, 8, 8192], P('box', 'spec', 'neuron')
The draws below stay inside these ranges and needn't reach their ends.
Inputs may be any that keep to these rules, and one draw needn't show every extreme that they name: `upper_bound`: positive. `lower_depth`: positive.
All inputs are finite; a program needn't handle non-finite values.
Results may differ from the reference program's by a relative error of at most 0.0095.
Values may be sent and summed in bfloat16 or wider, within the bound.
A program may use at most 64 MiB of HBM per device.

```python
import jax
import jax.numpy as jnp

D = 8192
SPECS = 8
BOXES = 96


def bound_values(key):
    ramp = 1.0 + 2.0 * jnp.arange(D, dtype=jnp.float32) / float(D - 1)
    base = jnp.exp(jax.random.uniform(key, (BOXES, D), jnp.float32, jnp.log(0.2), jnp.log(2.0)))
    return (base * ramp[None, :]).astype(jnp.float32)


def draw_upper_bound(key, part):
    return bound_values(jax.random.fold_in(key, 11))


def draw_lower_depth(key, part):
    return bound_values(jax.random.fold_in(key, 23))


def touch_ends(values, stream_key, least, high):
    longest = values.shape.index(max(values.shape))
    spots = []
    for shift in (0, 1):
        where = [jax.random.randint(jax.random.fold_in(stream_key, axis), (), 0, length) for axis, length in enumerate(values.shape)]
        where[longest] = (where[longest] + shift) % values.shape[longest]
        spots.append(tuple(where))
    return values.at[spots[0]].set(least).at[spots[1]].set(high)


def spiked(values, stream_key, source, target, shards_of, factor):
    owner, partner = [(jnp.arange(values.shape[position]) // (values.shape[position] // shards_of)).reshape([-1 if axis == position else 1 for axis in range(values.ndim)]) for position in (source, target)]
    chosen = jax.random.permutation(stream_key, shards_of)[partner]
    strong = (owner == chosen) | (owner == (partner + shards_of // 2) % shards_of)
    return jnp.where(strong, factor * values, values)


def block_scale(stream_key, extent, shards, smallest, largest):
    def one(axis_at, blocks):
        steps = jax.random.uniform(jax.random.fold_in(jax.random.fold_in(stream_key, 6), axis_at), (blocks,), jnp.float32, smallest / len(shards), largest / len(shards))
        return jnp.repeat(jnp.exp(steps), extent[axis_at] // blocks).reshape((-1,) + (1,) * (len(extent) - axis_at - 1))

    level = one(*shards[0])
    for cut in shards[1:]:
        level = level * one(*cut)
    return level


def scatter_about(stream_key, dims, scale, limit, shards=(), held_as=jnp.bfloat16):
    entries = jax.random.normal(stream_key, dims, jnp.float32) * scale
    if len(shards) > 0:
        entries = block_scale(stream_key, dims, shards, -0.22, 0.18) * entries
    return jnp.clip(entries, min=-limit, max=limit).astype(held_as)


def bell_draw_with(rng, shape, spread, most, split, heavy, kind=jnp.bfloat16):
    result = spread * jax.random.normal(rng, shape, jnp.float32)
    if split:
        result = result * block_scale(rng, shape, split, -0.22, 0.18)
    return jnp.clip(spiked(result, jax.random.fold_in(rng, 3), *heavy), -most, most).astype(kind)


def setup_inputs(seed: int = 0) -> dict:
    arg_keys = jax.random.split(jax.random.key(seed), 8)
    return {
        "coeff": scatter_about(arg_keys[0], (BOXES, SPECS, D), 1.0, 6.0, ((0, 4), (1, 2), (2, 4))),
        "weight": bell_draw_with(arg_keys[1], (D, D), D ** -0.5, 0.09375, ((0, 4), (1, 2)), (0, 1, 4, 2.0)),
        "upper_bound": draw_upper_bound(jax.random.fold_in(arg_keys[7], 71), 0),
        "lower_depth": draw_lower_depth(jax.random.fold_in(arg_keys[7], 71), 0),
        "slopes": jnp.clip(1.0 * jax.random.uniform(arg_keys[4], (BOXES, D), jnp.float32) ** block_scale(arg_keys[4], (BOXES, D), ((0, 4), (1, 4)), -0.2, 0.2), 0.0, 1.0),
        "state": touch_ends(jax.random.randint(arg_keys[5], (BOXES, D), 0, 3), jax.random.fold_in(arg_keys[5], 1), 0, 2).astype(jnp.int32),
        "adjoint": scatter_about(arg_keys[6], (BOXES, SPECS, D), 1.0, 6.0, ((0, 4), (1, 2), (2, 4))),
    }


def reference(coeff, weight, upper_bound, lower_depth, slopes, state, adjoint):
    rows = coeff.reshape(BOXES * SPECS, D)
    pre = jnp.dot(rows, weight, preferred_element_type=jnp.float32).reshape(BOXES, SPECS, D)
    upper3 = upper_bound[:, None, :]
    depth3 = lower_depth[:, None, :]
    upper_slope = upper3 / (upper3 + depth3)
    intercept = upper3 * depth3 / (upper3 + depth3)
    unstable = (state == 2)[:, None, :]
    active = (state == 1)[:, None, :]
    alpha3 = slopes[:, None, :]
    positive = jnp.maximum(pre, 0.0)
    negative = jnp.minimum(pre, 0.0)
    relaxed = jnp.where(unstable, alpha3 * positive + upper_slope * negative, jnp.where(active, pre, 0.0))
    new_coeff = relaxed.astype(jnp.bfloat16)
    offset = jnp.sum(jnp.where(unstable, negative * intercept, 0.0), axis=2) * (float(D) ** -0.5)
    cotangent = adjoint.astype(jnp.float32)
    factor = jnp.where(unstable, jnp.where(pre > 0.0, alpha3, upper_slope), jnp.where(active, 1.0, 0.0))
    grad_pre = (cotangent * factor).astype(jnp.bfloat16)
    slope_grad = jnp.sum(jnp.where(unstable, cotangent * positive, 0.0), axis=1)
    back = jnp.dot(grad_pre.reshape(BOXES * SPECS, D), weight.T, preferred_element_type=jnp.float32)
    coeff_grad = back.astype(jnp.bfloat16).reshape(BOXES, SPECS, D)
    return (new_coeff, offset, slope_grad, coeff_grad)
```

```python
import functools

import jax
import jax.numpy as jnp
from jax import lax
from jax.experimental import pallas as pl
from jax.experimental.pallas import tpu as pltpu
from jax.sharding import PartitionSpec as P

MESH = pl.DeviceIdType.MESH
F32 = jnp.float32
BF16 = jnp.bfloat16


def kernel(
    n, boxes, specs, tile, scale,
    coeff, weight, upper, depth, slopes, state, adjoint,
    new_coeff, offset, slope_grad, coeff_grad,
    held, other, mine, theirs, crossed, parts, params, t_params, t_adjoint, cotan,
    nc_out, nc_in, sg_out, sg_in, kept, away, back, off_part, offs,
    w_sem, a_sem, t_send, t_recv, c_send, c_recv, b_send, b_recv, g_send, g_recv, f_send,
    n_sem, s_send, s_recv, e_send, e_recv, o_send, o_recv,
):
    me, sp = lax.axis_index("neuron"), lax.axis_index("spec")
    h = n // 2
    per_core = h // 2
    core, chip = lax.rem(me, 2), lax.div(me, 2)
    mate = me + 1 - 2 * core
    half = lax.div(me, h)
    home = sp * h + lax.rem(me, h)
    fixed = half == sp
    rows, width = coeff.shape
    tiles = width // tile

    def remote(src, dst, send, recv, neuron, spec):
        return pltpu.make_async_remote_copy(
            src_ref=src, dst_ref=dst, send_sem=send, recv_sem=recv,
            device_id={"neuron": neuron, "spec": spec}, device_id_type=MESH,
        )

    def order(k):
        j = lax.rem(k, per_core)
        return 2 * j + jnp.where(k < per_core, 1 - core, core)

    def columns(q, t):
        return pl.ds(pl.multiple_of(q * width + t * tile, tile), tile)

    def load(k):
        q, t = order(lax.div(k, tiles)), lax.rem(k, tiles)
        return pltpu.make_async_copy(
            weight.at[:, columns(q, t)], held.at[:, columns(q, t)], w_sem.at[k]
        )

    @pl.loop(0, h * tiles)
    def _(k):
        load(k).start()

    barrier = pltpu.get_barrier_semaphore()
    for d in range(1, 2 * n):
        flat = lax.rem(me * 2 + sp + d, 2 * n)
        pl.semaphore_signal(
            barrier, inc=1,
            device_id={"neuron": lax.div(flat, 2), "spec": lax.rem(flat, 2)},
            device_id_type=MESH,
        )

    up = upper[...]
    unstable = state[...] == 2
    solid = jnp.where(state[...] == 1, 1.0, 0.0)
    params[...] = jnp.concatenate(
        [
            jnp.where(unstable, slopes[...], solid),
            jnp.where(unstable, up / (up + depth[...]), solid),
        ],
        axis=0,
    ).astype(BF16)
    pl.semaphore_wait(barrier, 2 * n - 1)

    a_copy = remote(coeff, other, a_sem.at[0], a_sem.at[1], me, 1 - sp)
    a_copy.start()
    t_copies = [
        remote(adjoint, t_adjoint, t_send.at[0], t_recv.at[0], home, half),
        remote(params, t_params, t_send.at[1], t_recv.at[1], home, half),
    ]
    t_local = [
        pltpu.make_async_copy(adjoint, t_adjoint, t_recv.at[0]),
        pltpu.make_async_copy(params, t_params, t_recv.at[1]),
    ]

    def start_either(far, near):
        @pl.when(fixed)
        def _():
            near.start()

        @pl.when(jnp.logical_not(fixed))
        def _():
            far.start()

    def wait_either(far, near):
        @pl.when(fixed)
        def _():
            near.wait()

        @pl.when(jnp.logical_not(fixed))
        def _():
            far.wait()

    for far, near in zip(t_copies, t_local):
        start_either(far, near)

    def core_copy(st, j):
        return remote(
            theirs.at[st, j], crossed.at[st, j], c_send.at[st, j], c_recv.at[st, j], mate, sp
        )

    def part_copy(st, j):
        spec_half = sp if st == 0 else 1 - sp
        owner = spec_half * per_core + j
        return owner, remote(
            mine.at[st, j], parts.at[chip], b_send.at[st, j], b_recv.at[chip],
            owner * 2 + core, sp,
        )

    for st in range(2):
        if st == 1:
            a_copy.wait()
        rows_in = coeff if st == 0 else other

        @pl.loop(0, per_core * tiles)
        def _(k):
            j, t = lax.div(k, tiles), lax.rem(k, tiles)
            if st == 0:
                load(k).wait()
            theirs[st, j, :, columns(0, t)] = jnp.dot(
                rows_in[...], held[:, columns(2 * j + 1 - core, t)], preferred_element_type=F32
            )

        for j in range(per_core):
            core_copy(st, j).start()

        @pl.loop(0, per_core * tiles)
        def _(k):
            j, t = lax.div(k, tiles), lax.rem(k, tiles)
            if st == 0:
                load(k + per_core * tiles).wait()
            mine[st, j, :, columns(0, t)] = jnp.dot(
                rows_in[...], held[:, columns(2 * j + core, t)], preferred_element_type=F32
            )

        for j in range(per_core):
            core_copy(st, j).wait()
            mine[st, j] = mine[st, j] + crossed[st, j]
            owner, copy = part_copy(st, j)

            @pl.when(owner != chip)
            def _():
                copy.start()

    own_stage = jnp.where(fixed, 0, 1)
    own_j = lax.rem(chip, per_core)
    for far, near in zip(t_copies, t_local):
        wait_either(far, near)
    for d in range(1, h):
        source = lax.rem(chip + d, h)
        pltpu.make_async_remote_copy(
            src_ref=mine.at[0, 0], dst_ref=parts.at[source], send_sem=b_send.at[0, 0],
            recv_sem=b_recv.at[source], device_id={"neuron": mate, "spec": sp},
            device_id_type=MESH,
        ).wait_recv()

    @pl.loop(0, tiles)
    def _(t):
        cols = columns(0, t)
        pre = mine[own_stage, own_j, :, cols]
        for d in range(1, h):
            pre = pre + parts[lax.rem(chip + d, h), :, cols]
        both = t_params[:, cols].astype(F32)
        low = jnp.concatenate([both[:boxes]] * specs, axis=0)
        high = jnp.concatenate([both[boxes:]] * specs, axis=0)
        cot = t_adjoint[:, cols].astype(F32)
        positive = jnp.maximum(pre, 0.0)
        cotan[me, :, cols] = (cot * jnp.where(pre > 0.0, low, high)).astype(BF16)
        nc_out[:, cols] = (low * positive + high * jnp.minimum(pre, 0.0)).astype(BF16)
        terms = cot * positive
        total = terms[:boxes]
        for s in range(1, specs):
            total = total + terms[s * boxes : (s + 1) * boxes]
        sg_out[:, cols] = jnp.concatenate(
            [total, jnp.zeros((sg_out.shape[0] - boxes, tile), F32)], axis=0
        ).astype(BF16)

    def g_copy(p):
        return remote(
            cotan.at[me], cotan.at[me], g_send.at[p], g_recv.at[me], p * 2 + core, sp
        )

    def own_core_copy():
        return remote(cotan.at[me], cotan.at[me], g_send.at[chip], g_recv.at[me], mate, sp)

    for d in range(1, h):
        g_copy(lax.rem(chip + d, h)).start()
    own_core_copy().start()
    nc_far = remote(nc_out, nc_in, n_sem.at[0], n_sem.at[1], home, half)
    nc_near = pltpu.make_async_copy(nc_out, nc_in, n_sem.at[1])
    start_either(nc_far, nc_near)
    sg_far = remote(sg_out, sg_in.at[half], s_send.at[0], s_recv.at[half], home, half)
    sg_near = pltpu.make_async_copy(sg_out, sg_in.at[half], s_recv.at[half])
    start_either(sg_far, sg_near)
    sg_side = remote(sg_out, sg_in.at[half], s_send.at[1], s_recv.at[half], home, 1 - half)
    sg_side.start()

    def arrival(i):
        return pltpu.make_async_remote_copy(
            src_ref=cotan.at[i], dst_ref=cotan.at[i], send_sem=f_send.at[0],
            recv_sem=g_recv.at[i], device_id={"neuron": mate, "spec": sp}, device_id_type=MESH,
        )

    def forward(p):
        i = p * 2 + core
        return remote(cotan.at[i], cotan.at[i], f_send.at[p], g_recv.at[i], mate, sp)

    def e_copy(t):
        return remote(
            away.at[:, columns(0, t)], back.at[:, columns(0, t)], e_send.at[t], e_recv.at[t],
            me, 1 - sp,
        )

    def backward(spec_half):
        @pl.loop(0, tiles)
        def _(t):
            line = pl.ds(pl.multiple_of(t * tile, tile), tile)
            total = jnp.zeros((rows, tile), F32)
            for q in range(h):
                total = total + lax.dot_general(
                    cotan[spec_half * h + q], held[line, q * width : (q + 1) * width],
                    (((1,), (1,)), ((), ())), preferred_element_type=F32,
                )

            @pl.when(spec_half == sp)
            def _():
                kept[:, columns(0, t)] = total

            @pl.when(spec_half != sp)
            def _():
                away[:, columns(0, t)] = total.astype(BF16)
                e_copy(t).start()

    own_first = half * per_core
    other_first = (1 - half) * per_core
    for first, skip in ((own_first, True), (other_first, False)):
        for j in range(per_core):
            p = first + j

            def take(p=p):
                arrival(p * 2 + core).wait_recv()
                forward(p).start()

            if skip:
                pl.when(p != chip)(take)
            else:
                take()
        for j in range(per_core):
            arrival((first + j) * 2 + 1 - core).wait_recv()
        backward(half if skip else 1 - half)

    wait_either(nc_far, nc_near)
    off_part[...] = jnp.zeros_like(off_part)

    @pl.loop(0, tiles)
    def _(t):
        cols = columns(0, t)
        value = nc_in[:, cols]
        new_coeff[:, cols] = value
        bound = jnp.where(state[:, cols] == 2, depth[:, cols], 0.0) * scale
        terms = jnp.minimum(value.astype(F32), 0.0) * jnp.concatenate([bound] * specs, axis=0)
        total = terms[:, :128]
        for c in range(1, tile // 128):
            total = total + terms[:, c * 128 : (c + 1) * 128]
        off_part[:rows, :] += total

    offs[me] = lax.dot_general(
        jnp.ones((8, 128), F32), off_part[...], (((1,), (1,)), ((), ())),
        precision=lax.Precision.HIGHEST, preferred_element_type=F32,
    )

    def o_copy(i):
        return remote(offs.at[me], offs.at[me], o_send.at[i], o_recv.at[me], i, sp)

    for d in range(1, n):
        o_copy(lax.rem(me + d, n)).start()

    wait_either(sg_far, sg_near)
    sg_side.wait_send()
    pltpu.make_async_remote_copy(
        src_ref=sg_out, dst_ref=sg_in.at[1 - half], send_sem=s_send.at[1],
        recv_sem=s_recv.at[1 - half], device_id={"neuron": mate, "spec": sp},
        device_id_type=MESH,
    ).wait_recv()
    both = sg_in[0].astype(F32)[:boxes] + sg_in[1].astype(F32)[:boxes]
    slope_grad[...] = jnp.where(state[...] == 2, both, 0.0)

    for t in range(tiles):
        e_copy(t).wait()
        cols = columns(0, t)
        coeff_grad[:, cols] = (kept[:, cols] + back[:, cols].astype(F32)).astype(BF16)

    for d in range(1, n):
        i = lax.rem(me + d, n)
        pltpu.make_async_remote_copy(
            src_ref=offs.at[i], dst_ref=offs.at[i], send_sem=o_send.at[me],
            recv_sem=o_recv.at[i], device_id={"neuron": mate, "spec": sp}, device_id_type=MESH,
        ).wait_recv()
    result = offs[0]
    for i in range(1, n):
        result = result + offs[i]
    offset[...] = result

    for d in range(1, n):
        o_copy(lax.rem(me + d, n)).wait_send()
    for d in range(1, h):
        p = lax.rem(chip + d, h)
        g_copy(p).wait_send()
        forward(p).wait_send()
    own_core_copy().wait_send()
    for st in range(2):
        for j in range(per_core):
            owner, copy = part_copy(st, j)

            @pl.when(owner != chip)
            def _():
                copy.wait_send()


def shards(coeff, weight, upper_bound, lower_depth, slopes, state, adjoint):
    boxes, specs, width = coeff.shape
    n = lax.axis_size("neuron")
    h, rows = n // 2, boxes * specs
    per_core = h // 2
    total = width * n
    tile = min(width, 512)
    tiles = width // tile
    flat = lambda v: jnp.transpose(v, (1, 0, 2)).reshape(rows, width)
    dma = lambda *s: pltpu.SemaphoreType.DMA(s)
    vmem = pl.BlockSpec(memory_space=pltpu.VMEM)
    nc, offset, slope_grad, grad = pl.pallas_call(
        functools.partial(kernel, n, boxes, specs, tile, float(total) ** -0.5),
        out_shape=(
            jax.ShapeDtypeStruct((rows, width), BF16),
            jax.ShapeDtypeStruct((8, 128), F32),
            jax.ShapeDtypeStruct((boxes, width), F32),
            jax.ShapeDtypeStruct((rows, width), BF16),
        ),
        in_specs=[vmem, pl.BlockSpec(memory_space=pl.ANY)] + [vmem] * 5,
        out_specs=(vmem,) * 4,
        scratch_shapes=[
            pltpu.VMEM(weight.shape, BF16),
            pltpu.VMEM((rows, width), BF16),
            pltpu.VMEM((2, per_core, rows, width), F32),
            pltpu.VMEM((2, per_core, rows, width), F32),
            pltpu.VMEM((2, per_core, rows, width), F32),
            pltpu.VMEM((h, rows, width), F32),
            pltpu.VMEM((2 * boxes, width), BF16),
            pltpu.VMEM((2 * boxes, width), BF16),
            pltpu.VMEM((rows, width), BF16),
            pltpu.VMEM((n, rows, width), BF16),
            pltpu.VMEM((rows, width), BF16),
            pltpu.VMEM((rows, width), BF16),
            pltpu.VMEM((-(-boxes // 16) * 16, width), BF16),
            pltpu.VMEM((2, -(-boxes // 16) * 16, width), BF16),
            pltpu.VMEM((rows, width), F32),
            pltpu.VMEM((rows, width), BF16),
            pltpu.VMEM((rows, width), BF16),
            pltpu.VMEM((128, 128), F32),
            pltpu.VMEM((n, 8, 128), F32),
            dma(h * tiles), dma(2), dma(2), dma(2),
            dma(2, per_core), dma(2, per_core), dma(2, per_core), dma(h),
            dma(h), dma(n), dma(h),
            dma(2), dma(2), dma(2), dma(tiles), dma(tiles), dma(n), dma(n),
        ],
        compiler_params=pltpu.CompilerParams(
            collective_id=0, has_side_effects=True, vmem_limit_bytes=48 * 1024 * 1024
        ),
        cost_estimate=pl.CostEstimate(
            flops=8 * rows * weight.size, bytes_accessed=2 * weight.size, transcendentals=0
        ),
    )(
        flat(coeff), weight, upper_bound, lower_depth, slopes, state, flat(adjoint),
    )
    wide = lambda v: jnp.transpose(v.reshape(specs, boxes, width), (1, 0, 2))
    return (
        wide(nc), jnp.transpose(offset[0, :rows].reshape(specs, boxes)), slope_grad, wide(grad),
    )


def solution(mesh):
    return jax.shard_map(
        shards,
        mesh=mesh,
        in_specs=(
            P("box", "spec", "neuron"),
            P("neuron", "spec"),
            P("box", "neuron"),
            P("box", "neuron"),
            P("box", "neuron"),
            P("box", "neuron"),
            P("box", "spec", "neuron"),
        ),
        out_specs=(
            P("box", "spec", "neuron"),
            P("box", "spec"),
            P("box", "neuron"),
            P("box", "spec", "neuron"),
        ),
        check_vma=False,
    )
```

```python
import functools

import jax
import jax.numpy as jnp
from jax import lax
from jax.experimental import pallas as pl
from jax.experimental.pallas import tpu as pltpu
from jax.sharding import PartitionSpec as P

MESH = pl.DeviceIdType.MESH
F32 = jnp.float32
BF16 = jnp.bfloat16


def kernel(
    n, boxes, specs, tile, scale,
    coeff, weight, upper_in, depth_in, slopes_in, state_in, adjoint,
    new_coeff, offset, slope_grad, coeff_grad,
    upper, depth, slopes, state, held, other, mine, theirs, crossed, parts, params, t_params, t_adjoint, cotan,
    nc_out, nc_in, sg_out, sg_in, kept, away, back, off_part, offs,
    i_sem, w_sem, a_sem, t_send, t_recv, c_send, c_recv, b_send, b_recv, g_send, g_recv, f_send,
    n_sem, s_send, s_recv, e_send, e_recv, o_send, o_recv,
):
    me, sp = lax.axis_index("neuron"), lax.axis_index("spec")
    h = n // 2
    per_core = h // 2
    core, chip = lax.rem(me, 2), lax.div(me, 2)
    mate = me + 1 - 2 * core
    half = 1 - lax.div(me, h)
    home = sp * h + lax.rem(me, h)
    owner, owner_spec = (1 - sp) * h + lax.rem(me, h), lax.div(me, h)
    rows, width = coeff.shape
    tiles = width // tile

    def remote(src, dst, send, recv, neuron, spec):
        return pltpu.make_async_remote_copy(
            src_ref=src, dst_ref=dst, send_sem=send, recv_sem=recv,
            device_id={"neuron": neuron, "spec": spec}, device_id_type=MESH,
        )

    def order(k):
        j = lax.rem(k, per_core)
        return 2 * j + jnp.where(k < per_core, 1 - core, core)

    def columns(q, t):
        return pl.ds(pl.multiple_of(q * width + t * tile, tile), tile)

    def load(k):
        q, t = order(lax.div(k, tiles)), lax.rem(k, tiles)
        return pltpu.make_async_copy(
            weight.at[:, columns(q, t)], held.at[:, columns(q, t)], w_sem.at[k]
        )

    bounds = [
        pltpu.make_async_copy(src, dst, i_sem.at[k])
        for k, (src, dst) in enumerate(
            ((upper_in, upper), (depth_in, depth), (slopes_in, slopes), (state_in, state))
        )
    ]
    for copy in bounds:
        copy.start()

    @pl.loop(0, h * tiles)
    def _(k):
        load(k).start()

    barrier = pltpu.get_barrier_semaphore()
    for d in range(1, 2 * n):
        flat = lax.rem(me * 2 + sp + d, 2 * n)
        pl.semaphore_signal(
            barrier, inc=1,
            device_id={"neuron": lax.div(flat, 2), "spec": lax.rem(flat, 2)},
            device_id_type=MESH,
        )

    pl.semaphore_wait(barrier, 2 * n - 1)

    a_copy = remote(coeff, other, a_sem.at[0], a_sem.at[1], me, 1 - sp)
    a_copy.start()
    adjoint_copy = remote(adjoint, t_adjoint, t_send.at[0], t_recv.at[0], owner, owner_spec)
    adjoint_copy.start()
    for copy in bounds:
        copy.wait()
    up = upper[...]
    unstable = state[...] == 2
    solid = jnp.where(state[...] == 1, 1.0, 0.0)
    params[...] = jnp.concatenate(
        [
            jnp.where(unstable, slopes[...], solid),
            jnp.where(unstable, up / (up + depth[...]), solid),
        ],
        axis=0,
    ).astype(BF16)
    params_copy = remote(params, t_params, t_send.at[1], t_recv.at[1], owner, owner_spec)
    params_copy.start()

    def core_copy(st, j, t):
        cols = columns(0, t)
        return remote(
            theirs.at[st, j, :, cols], crossed.at[st, j, :, cols],
            c_send.at[st, j, t], c_recv.at[st, j, t], mate, sp,
        )

    def part_copy(st, j, t):
        spec_half = sp if st == 0 else 1 - sp
        target = (1 - spec_half) * per_core + j
        cols = columns(0, t)
        return target, remote(
            mine.at[st, j, :, cols], parts.at[chip, :, cols],
            b_send.at[st, j, t], b_recv.at[chip, t], target * 2 + core, sp,
        )

    for st in range(2):
        if st == 1:
            a_copy.wait()
        rows_in = coeff if st == 0 else other

        @pl.loop(0, per_core * tiles)
        def _(k):
            j, t = lax.div(k, tiles), lax.rem(k, tiles)
            if st == 0:
                load(k).wait()
            theirs[st, j, :, columns(0, t)] = jnp.dot(
                rows_in[...], held[:, columns(2 * j + 1 - core, t)], preferred_element_type=F32
            )
            core_copy(st, j, t).start()

        @pl.loop(0, per_core * tiles)
        def _(k):
            j, t = lax.div(k, tiles), lax.rem(k, tiles)
            cols = columns(0, t)
            if st == 0:
                load(k + per_core * tiles).wait()
            total = jnp.dot(
                rows_in[...], held[:, columns(2 * j + core, t)], preferred_element_type=F32
            )
            core_copy(st, j, t).wait()
            mine[st, j, :, cols] = total + crossed[st, j, :, cols]
            target, copy = part_copy(st, j, t)

            @pl.when(target != chip)
            def _():
                copy.start()

    own_stage = jnp.where(half == sp, 0, 1)
    own_j = lax.rem(chip, per_core)
    adjoint_copy.wait()
    params_copy.wait()

    def g_copy(p, t):
        cols = columns(0, t)
        return remote(
            cotan.at[me, :, cols], cotan.at[me, :, cols],
            g_send.at[p, t], g_recv.at[me, t], p * 2 + core, sp,
        )

    def own_core_copy(t):
        cols = columns(0, t)
        return remote(
            cotan.at[me, :, cols], cotan.at[me, :, cols],
            g_send.at[chip, t], g_recv.at[me, t], mate, sp,
        )

    @pl.loop(0, tiles)
    def _(t):
        cols = columns(0, t)
        pre = mine[own_stage, own_j, :, cols]
        for d in range(1, h):
            source = lax.rem(chip + d, h)
            pltpu.make_async_remote_copy(
                src_ref=mine.at[0, 0, :, cols], dst_ref=parts.at[source, :, cols],
                send_sem=b_send.at[0, 0, t], recv_sem=b_recv.at[source, t],
                device_id={"neuron": mate, "spec": sp}, device_id_type=MESH,
            ).wait_recv()
            pre = pre + parts[source, :, cols]
        both = t_params[:, cols].astype(F32)
        low = jnp.concatenate([both[:boxes]] * specs, axis=0)
        high = jnp.concatenate([both[boxes:]] * specs, axis=0)
        cot = t_adjoint[:, cols].astype(F32)
        positive = jnp.maximum(pre, 0.0)
        cotan[me, :, cols] = (cot * jnp.where(pre > 0.0, low, high)).astype(BF16)
        nc_out[:, cols] = (low * positive + high * jnp.minimum(pre, 0.0)).astype(BF16)
        terms = cot * positive
        total = terms[:boxes]
        for s in range(1, specs):
            total = total + terms[s * boxes : (s + 1) * boxes]
        sg_out[:, cols] = jnp.concatenate(
            [total, jnp.zeros((sg_out.shape[0] - boxes, tile), F32)], axis=0
        ).astype(BF16)

        for d in range(1, h):
            g_copy(lax.rem(chip + d, h), t).start()
        own_core_copy(t).start()

    nc_copy = remote(nc_out, nc_in, n_sem.at[0], n_sem.at[1], home, half)
    nc_copy.start()
    sg_copy = remote(sg_out, sg_in.at[half], s_send.at[0], s_recv.at[half], home, half)
    sg_copy.start()
    sg_far = remote(sg_out, sg_in.at[half], s_send.at[1], s_recv.at[half], home, 1 - half)
    sg_near = pltpu.make_async_copy(sg_out, sg_in.at[half], s_recv.at[half])
    fixed = home == me

    @pl.when(fixed)
    def _():
        sg_near.start()

    @pl.when(jnp.logical_not(fixed))
    def _():
        sg_far.start()

    def arrival(i, t):
        cols = columns(0, t)
        return pltpu.make_async_remote_copy(
            src_ref=cotan.at[i, :, cols], dst_ref=cotan.at[i, :, cols], send_sem=f_send.at[0, t],
            recv_sem=g_recv.at[i, t], device_id={"neuron": mate, "spec": sp},
            device_id_type=MESH,
        )

    def forward(p, t):
        i = p * 2 + core
        cols = columns(0, t)
        return remote(
            cotan.at[i, :, cols], cotan.at[i, :, cols], f_send.at[p, t], g_recv.at[i, t], mate, sp
        )

    def e_copy(t):
        return remote(
            away.at[:, columns(0, t)], back.at[:, columns(0, t)], e_send.at[t], e_recv.at[t],
            me, 1 - sp,
        )

    def backward(spec_half):
        @pl.loop(0, tiles)
        def _(t):
            line = pl.ds(pl.multiple_of(t * tile, tile), tile)
            total = jnp.zeros((rows, tile), F32)
            for q in range(h):
                total = total + lax.dot_general(
                    cotan[(1 - spec_half) * h + q], held[line, q * width : (q + 1) * width],
                    (((1,), (1,)), ((), ())), preferred_element_type=F32,
                )

            @pl.when(spec_half == sp)
            def _():
                kept[:, columns(0, t)] = total

            @pl.when(spec_half != sp)
            def _():
                away[:, columns(0, t)] = total.astype(BF16)
                e_copy(t).start()

    for spec_half, skip in ((half, True), (1 - half, False)):
        first = (1 - spec_half) * per_core
        for j in range(per_core):
            p = first + j

            def take(p=p):
                @pl.loop(0, tiles)
                def _(t):
                    arrival(p * 2 + core, t).wait_recv()
                    forward(p, t).start()

            if skip:
                pl.when(p != chip)(take)
            else:
                take()

        @pl.loop(0, per_core * tiles)
        def _(k):
            p = first + lax.div(k, tiles)
            arrival(p * 2 + 1 - core, lax.rem(k, tiles)).wait_recv()

        backward(spec_half)

    nc_copy.wait()
    off_part[...] = jnp.zeros_like(off_part)

    @pl.loop(0, tiles)
    def _(t):
        cols = columns(0, t)
        value = nc_in[:, cols]
        new_coeff[:, cols] = value
        bound = jnp.where(state[:, cols] == 2, depth[:, cols], 0.0) * scale
        terms = jnp.minimum(value.astype(F32), 0.0) * jnp.concatenate([bound] * specs, axis=0)
        total = terms[:, :128]
        for c in range(1, tile // 128):
            total = total + terms[:, c * 128 : (c + 1) * 128]
        off_part[:rows, :] += total

    offs[me] = lax.dot_general(
        jnp.ones((8, 128), F32), off_part[...], (((1,), (1,)), ((), ())),
        precision=lax.Precision.HIGHEST, preferred_element_type=F32,
    )

    def o_copy(i):
        return remote(offs.at[me], offs.at[me], o_send.at[i], o_recv.at[me], i, sp)

    for d in range(1, n):
        o_copy(lax.rem(me + d, n)).start()

    def sg_arrival(k):
        return pltpu.make_async_remote_copy(
            src_ref=sg_out, dst_ref=sg_in.at[k], send_sem=s_send.at[1],
            recv_sem=s_recv.at[k], device_id={"neuron": mate, "spec": sp}, device_id_type=MESH,
        )

    sg_copy.wait_send()

    @pl.when(jnp.logical_not(fixed))
    def _():
        sg_far.wait_send()

    for k in range(2):
        sg_arrival(k).wait_recv()
    both = sg_in[0].astype(F32)[:boxes] + sg_in[1].astype(F32)[:boxes]
    slope_grad[...] = jnp.where(state[...] == 2, both, 0.0)

    for t in range(tiles):
        e_copy(t).wait()
        cols = columns(0, t)
        coeff_grad[:, cols] = (kept[:, cols] + back[:, cols].astype(F32)).astype(BF16)

    for d in range(1, n):
        i = lax.rem(me + d, n)
        pltpu.make_async_remote_copy(
            src_ref=offs.at[i], dst_ref=offs.at[i], send_sem=o_send.at[me],
            recv_sem=o_recv.at[i], device_id={"neuron": mate, "spec": sp}, device_id_type=MESH,
        ).wait_recv()
    result = offs[0]
    for i in range(1, n):
        result = result + offs[i]
    offset[...] = result

    for d in range(1, n):
        o_copy(lax.rem(me + d, n)).wait_send()
    @pl.loop(0, tiles)
    def _(t):
        for d in range(1, h):
            p = lax.rem(chip + d, h)
            g_copy(p, t).wait_send()
            forward(p, t).wait_send()
        own_core_copy(t).wait_send()
        for st in range(2):
            for j in range(per_core):
                target, copy = part_copy(st, j, t)

                @pl.when(target != chip)
                def _():
                    copy.wait_send()


def shards(coeff, weight, upper_bound, lower_depth, slopes, state, adjoint):
    boxes, specs, width = coeff.shape
    n = lax.axis_size("neuron")
    h, rows = n // 2, boxes * specs
    per_core = h // 2
    total = width * n
    tile = min(width, 512)
    tiles = width // tile
    flat = lambda v: jnp.transpose(v, (1, 0, 2)).reshape(rows, width)
    dma = lambda *s: pltpu.SemaphoreType.DMA(s)
    vmem = pl.BlockSpec(memory_space=pltpu.VMEM)
    nc, offset, slope_grad, grad = pl.pallas_call(
        functools.partial(kernel, n, boxes, specs, tile, float(total) ** -0.5),
        out_shape=(
            jax.ShapeDtypeStruct((rows, width), BF16),
            jax.ShapeDtypeStruct((8, 128), F32),
            jax.ShapeDtypeStruct((boxes, width), F32),
            jax.ShapeDtypeStruct((rows, width), BF16),
        ),
        in_specs=[vmem] + [pl.BlockSpec(memory_space=pltpu.HBM)] * 5 + [vmem],
        out_specs=(vmem,) * 4,
        scratch_shapes=[
            pltpu.VMEM((boxes, width), F32),
            pltpu.VMEM((boxes, width), F32),
            pltpu.VMEM((boxes, width), F32),
            pltpu.VMEM((boxes, width), jnp.int32),
            pltpu.VMEM(weight.shape, BF16),
            pltpu.VMEM((rows, width), BF16),
            pltpu.VMEM((2, per_core, rows, width), F32),
            pltpu.VMEM((2, per_core, rows, width), F32),
            pltpu.VMEM((2, per_core, rows, width), F32),
            pltpu.VMEM((h, rows, width), F32),
            pltpu.VMEM((2 * boxes, width), BF16),
            pltpu.VMEM((2 * boxes, width), BF16),
            pltpu.VMEM((rows, width), BF16),
            pltpu.VMEM((n, rows, width), BF16),
            pltpu.VMEM((rows, width), BF16),
            pltpu.VMEM((rows, width), BF16),
            pltpu.VMEM((-(-boxes // 16) * 16, width), BF16),
            pltpu.VMEM((2, -(-boxes // 16) * 16, width), BF16),
            pltpu.VMEM((rows, width), F32),
            pltpu.VMEM((rows, width), BF16),
            pltpu.VMEM((rows, width), BF16),
            pltpu.VMEM((128, 128), F32),
            pltpu.VMEM((n, 8, 128), F32),
            dma(4), dma(h * tiles), dma(2), dma(2), dma(2),
            dma(2, per_core, tiles), dma(2, per_core, tiles), dma(2, per_core, tiles),
            dma(h, tiles), dma(h, tiles), dma(n, tiles), dma(h, tiles),
            dma(2), dma(2), dma(2), dma(tiles), dma(tiles), dma(n), dma(n),
        ],
        compiler_params=pltpu.CompilerParams(
            collective_id=0, has_side_effects=True, vmem_limit_bytes=48 * 1024 * 1024
        ),
        cost_estimate=pl.CostEstimate(
            flops=8 * rows * weight.size, bytes_accessed=2 * weight.size, transcendentals=0
        ),
    )(
        flat(coeff), weight, upper_bound, lower_depth, slopes, state, flat(adjoint),
    )
    wide = lambda v: jnp.transpose(v.reshape(specs, boxes, width), (1, 0, 2))
    return (
        wide(nc), jnp.transpose(offset[0, :rows].reshape(specs, boxes)), slope_grad, wide(grad),
    )


def solution(mesh):
    return jax.shard_map(
        shards,
        mesh=mesh,
        in_specs=(
            P("box", "spec", "neuron"),
            P("neuron", "spec"),
            P("box", "neuron"),
            P("box", "neuron"),
            P("box", "neuron"),
            P("box", "neuron"),
            P("box", "spec", "neuron"),
        ),
        out_specs=(
            P("box", "spec", "neuron"),
            P("box", "spec"),
            P("box", "neuron"),
            P("box", "spec", "neuron"),
        ),
        check_vma=False,
    )
```

```python
import functools

import jax
import jax.numpy as jnp
from jax import lax
from jax.experimental import pallas as pl
from jax.experimental.pallas import tpu as pltpu
from jax.sharding import PartitionSpec as P

MESH = pl.DeviceIdType.MESH
F32 = jnp.float32
BF16 = jnp.bfloat16


def kernel(
    n, boxes, specs, tile, scale,
    coeff, weight, upper_in, depth_in, slopes_in, state_in, adjoint,
    new_coeff, offset, slope_grad, coeff_grad,
    upper, depth, slopes, state, held, other, mine, theirs, crossed, coded, scales, parts, part_scales, params, t_params, t_adjoint, cotan,
    nc_out, nc_in, sg_out, sg_in, kept, away, back, off_part, offs,
    i_sem, w_sem, a_sem, t_send, t_recv, c_send, c_recv, b_send, b_recv, d_send, d_recv, g_send, g_recv, f_send,
    n_sem, s_send, s_recv, e_send, e_recv, o_send, o_recv,
):
    me, sp = lax.axis_index("neuron"), lax.axis_index("spec")
    h = n // 2
    per_core = h // 2
    core, chip = lax.rem(me, 2), lax.div(me, 2)
    mate = me + 1 - 2 * core
    half = 1 - lax.div(me, h)
    home = sp * h + lax.rem(me, h)
    owner, owner_spec = (1 - sp) * h + lax.rem(me, h), lax.div(me, h)
    rows, width = coeff.shape
    tiles = width // tile

    def remote(src, dst, send, recv, neuron, spec):
        return pltpu.make_async_remote_copy(
            src_ref=src, dst_ref=dst, send_sem=send, recv_sem=recv,
            device_id={"neuron": neuron, "spec": spec}, device_id_type=MESH,
        )

    def order(k):
        j = lax.rem(k, per_core)
        return 2 * j + jnp.where(k < per_core, 1 - core, core)

    def columns(q, t):
        return pl.ds(pl.multiple_of(q * width + t * tile, tile), tile)

    def load(k):
        q, t = order(lax.div(k, tiles)), lax.rem(k, tiles)
        return pltpu.make_async_copy(
            weight.at[:, columns(q, t)], held.at[:, columns(q, t)], w_sem.at[k]
        )

    bounds = [
        pltpu.make_async_copy(src, dst, i_sem.at[k])
        for k, (src, dst) in enumerate(
            ((upper_in, upper), (depth_in, depth), (slopes_in, slopes), (state_in, state))
        )
    ]
    for copy in bounds:
        copy.start()

    @pl.loop(0, h * tiles)
    def _(k):
        load(k).start()

    barrier = pltpu.get_barrier_semaphore()
    for d in range(1, 2 * n):
        flat = lax.rem(me * 2 + sp + d, 2 * n)
        pl.semaphore_signal(
            barrier, inc=1,
            device_id={"neuron": lax.div(flat, 2), "spec": lax.rem(flat, 2)},
            device_id_type=MESH,
        )

    pl.semaphore_wait(barrier, 2 * n - 1)

    a_copy = remote(coeff, other, a_sem.at[0], a_sem.at[1], me, 1 - sp)
    a_copy.start()
    adjoint_copy = remote(adjoint, t_adjoint, t_send.at[0], t_recv.at[0], owner, owner_spec)
    adjoint_copy.start()
    for copy in bounds:
        copy.wait()
    up = upper[...]
    unstable = state[...] == 2
    solid = jnp.where(state[...] == 1, 1.0, 0.0)
    params[...] = jnp.concatenate(
        [
            jnp.where(unstable, slopes[...], solid),
            jnp.where(unstable, up / (up + depth[...]), solid),
        ],
        axis=0,
    ).astype(BF16)
    params_copy = remote(params, t_params, t_send.at[1], t_recv.at[1], owner, owner_spec)
    params_copy.start()

    def core_copy(st, j, t):
        cols = columns(0, t)
        return remote(
            theirs.at[st, j, :, cols], crossed.at[st, j, :, cols],
            c_send.at[st, j, t], c_recv.at[st, j, t], mate, sp,
        )

    def part_copy(st, j, t):
        spec_half = sp if st == 0 else 1 - sp
        target = (1 - spec_half) * per_core + j
        cols = columns(0, t)
        return target, remote(
            coded.at[st, j, :, cols], parts.at[chip, :, cols],
            b_send.at[st, j, t], b_recv.at[chip, t], target * 2 + core, sp,
        ), remote(
            scales.at[st, j, t], part_scales.at[chip, t],
            d_send.at[st, j, t], d_recv.at[chip, t], target * 2 + core, sp,
        )

    diagonal = lax.broadcasted_iota(jnp.int32, (rows, 128), 0) == lax.broadcasted_iota(
        jnp.int32, (rows, 128), 1
    )

    for st in range(2):
        if st == 1:
            a_copy.wait()
        rows_in = coeff if st == 0 else other

        @pl.loop(0, per_core * tiles)
        def _(k):
            j, t = lax.div(k, tiles), lax.rem(k, tiles)
            if st == 0:
                load(k).wait()
            theirs[st, j, :, columns(0, t)] = jnp.dot(
                rows_in[...], held[:, columns(2 * j + 1 - core, t)], preferred_element_type=F32
            )
            core_copy(st, j, t).start()

        @pl.loop(0, per_core * tiles)
        def _(k):
            j, t = lax.div(k, tiles), lax.rem(k, tiles)
            cols = columns(0, t)
            if st == 0:
                load(k + per_core * tiles).wait()
            total = jnp.dot(
                rows_in[...], held[:, columns(2 * j + core, t)], preferred_element_type=F32
            )
            core_copy(st, j, t).wait()
            total = total + crossed[st, j, :, cols]
            target, copy, scale_copy = part_copy(st, j, t)

            @pl.when(target == chip)
            def _():
                mine[:, cols] = total

            @pl.when(target != chip)
            def _():
                largest = jnp.maximum(jnp.max(jnp.abs(total), axis=1, keepdims=True), 1e-30)
                whole = jnp.round(total * (32766.0 / largest))
                coded[st, j, :, cols] = whole.astype(jnp.int32).astype(jnp.int16)
                step = jnp.where(diagonal, largest * (1.0 / 32766.0), 0.0)
                scales[st, j, t] = jnp.broadcast_to(jnp.sum(step, axis=0, keepdims=True), (8, 128))
                copy.start()
                scale_copy.start()

    adjoint_copy.wait()
    params_copy.wait()

    def g_copy(p, t):
        cols = columns(0, t)
        return remote(
            cotan.at[me, :, cols], cotan.at[me, :, cols],
            g_send.at[p, t], g_recv.at[me, t], p * 2 + core, sp,
        )

    def own_core_copy(t):
        cols = columns(0, t)
        return remote(
            cotan.at[me, :, cols], cotan.at[me, :, cols],
            g_send.at[chip, t], g_recv.at[me, t], mate, sp,
        )

    @pl.loop(0, tiles)
    def _(t):
        cols = columns(0, t)
        pre = mine[:, cols]
        for d in range(1, h):
            source = lax.rem(chip + d, h)
            pltpu.make_async_remote_copy(
                src_ref=coded.at[0, 0, :, cols], dst_ref=parts.at[source, :, cols],
                send_sem=b_send.at[0, 0, t], recv_sem=b_recv.at[source, t],
                device_id={"neuron": mate, "spec": sp}, device_id_type=MESH,
            ).wait_recv()
            pltpu.make_async_remote_copy(
                src_ref=scales.at[0, 0, t], dst_ref=part_scales.at[source, t],
                send_sem=d_send.at[0, 0, t], recv_sem=d_recv.at[source, t],
                device_id={"neuron": mate, "spec": sp}, device_id_type=MESH,
            ).wait_recv()
            step = jnp.where(diagonal, part_scales[source, t][:1], 0.0)
            step = jnp.sum(step, axis=1, keepdims=True)
            pre = pre + parts[source, :, cols].astype(jnp.int32).astype(F32) * step
        both = t_params[:, cols].astype(F32)
        low = jnp.concatenate([both[:boxes]] * specs, axis=0)
        high = jnp.concatenate([both[boxes:]] * specs, axis=0)
        cot = t_adjoint[:, cols].astype(F32)
        positive = jnp.maximum(pre, 0.0)
        cotan[me, :, cols] = (cot * jnp.where(pre > 0.0, low, high)).astype(BF16)
        nc_out[:, cols] = (low * positive + high * jnp.minimum(pre, 0.0)).astype(BF16)
        terms = cot * positive
        total = terms[:boxes]
        for s in range(1, specs):
            total = total + terms[s * boxes : (s + 1) * boxes]
        sg_out[:, cols] = jnp.concatenate(
            [total, jnp.zeros((sg_out.shape[0] - boxes, tile), F32)], axis=0
        ).astype(BF16)

        for d in range(1, h):
            g_copy(lax.rem(chip + d, h), t).start()
        own_core_copy(t).start()

    nc_copy = remote(nc_out, nc_in, n_sem.at[0], n_sem.at[1], home, half)
    nc_copy.start()
    sg_copy = remote(sg_out, sg_in.at[half], s_send.at[0], s_recv.at[half], home, half)
    sg_copy.start()
    sg_far = remote(sg_out, sg_in.at[half], s_send.at[1], s_recv.at[half], home, 1 - half)
    sg_near = pltpu.make_async_copy(sg_out, sg_in.at[half], s_recv.at[half])
    fixed = home == me

    @pl.when(fixed)
    def _():
        sg_near.start()

    @pl.when(jnp.logical_not(fixed))
    def _():
        sg_far.start()

    def arrival(i, t):
        cols = columns(0, t)
        return pltpu.make_async_remote_copy(
            src_ref=cotan.at[i, :, cols], dst_ref=cotan.at[i, :, cols], send_sem=f_send.at[0, t],
            recv_sem=g_recv.at[i, t], device_id={"neuron": mate, "spec": sp},
            device_id_type=MESH,
        )

    def forward(p, t):
        i = p * 2 + core
        cols = columns(0, t)
        return remote(
            cotan.at[i, :, cols], cotan.at[i, :, cols], f_send.at[p, t], g_recv.at[i, t], mate, sp
        )

    def e_copy(t):
        return remote(
            away.at[:, columns(0, t)], back.at[:, columns(0, t)], e_send.at[t], e_recv.at[t],
            me, 1 - sp,
        )

    def backward(spec_half):
        @pl.loop(0, tiles)
        def _(t):
            line = pl.ds(pl.multiple_of(t * tile, tile), tile)
            total = jnp.zeros((rows, tile), F32)
            for q in range(h):
                total = total + lax.dot_general(
                    cotan[(1 - spec_half) * h + q], held[line, q * width : (q + 1) * width],
                    (((1,), (1,)), ((), ())), preferred_element_type=F32,
                )

            @pl.when(spec_half == sp)
            def _():
                kept[:, columns(0, t)] = total

            @pl.when(spec_half != sp)
            def _():
                away[:, columns(0, t)] = total.astype(BF16)
                e_copy(t).start()

    for spec_half, skip in ((half, True), (1 - half, False)):
        first = (1 - spec_half) * per_core
        for j in range(per_core):
            p = first + j

            def take(p=p):
                @pl.loop(0, tiles)
                def _(t):
                    arrival(p * 2 + core, t).wait_recv()
                    forward(p, t).start()

            if skip:
                pl.when(p != chip)(take)
            else:
                take()

        @pl.loop(0, per_core * tiles)
        def _(k):
            p = first + lax.div(k, tiles)
            arrival(p * 2 + 1 - core, lax.rem(k, tiles)).wait_recv()

        backward(spec_half)

    nc_copy.wait()
    off_part[...] = jnp.zeros_like(off_part)

    @pl.loop(0, tiles)
    def _(t):
        cols = columns(0, t)
        value = nc_in[:, cols]
        new_coeff[:, cols] = value
        bound = jnp.where(state[:, cols] == 2, depth[:, cols], 0.0) * scale
        terms = jnp.minimum(value.astype(F32), 0.0) * jnp.concatenate([bound] * specs, axis=0)
        total = terms[:, :128]
        for c in range(1, tile // 128):
            total = total + terms[:, c * 128 : (c + 1) * 128]
        off_part[...] += total

    lane = lax.broadcasted_iota(jnp.int32, (boxes, 128), 1)
    result = jnp.zeros((boxes, 128), F32)
    for k in range(specs):
        one = jnp.sum(off_part[k * boxes : (k + 1) * boxes, :], axis=1, keepdims=True)
        result = result + jnp.where(lane == k, one, 0.0)
    offs[me] = result

    def o_copy(i):
        return remote(offs.at[me], offs.at[me], o_send.at[i], o_recv.at[me], i, sp)

    for d in range(1, n):
        o_copy(lax.rem(me + d, n)).start()

    def sg_arrival(k):
        return pltpu.make_async_remote_copy(
            src_ref=sg_out, dst_ref=sg_in.at[k], send_sem=s_send.at[1],
            recv_sem=s_recv.at[k], device_id={"neuron": mate, "spec": sp}, device_id_type=MESH,
        )

    sg_copy.wait_send()

    @pl.when(jnp.logical_not(fixed))
    def _():
        sg_far.wait_send()

    for k in range(2):
        sg_arrival(k).wait_recv()
    both = sg_in[0].astype(F32)[:boxes] + sg_in[1].astype(F32)[:boxes]
    slope_grad[...] = jnp.where(state[...] == 2, both, 0.0)

    for t in range(tiles):
        e_copy(t).wait()
        cols = columns(0, t)
        coeff_grad[:, cols] = (kept[:, cols] + back[:, cols].astype(F32)).astype(BF16)

    for d in range(1, n):
        i = lax.rem(me + d, n)
        pltpu.make_async_remote_copy(
            src_ref=offs.at[i], dst_ref=offs.at[i], send_sem=o_send.at[me],
            recv_sem=o_recv.at[i], device_id={"neuron": mate, "spec": sp}, device_id_type=MESH,
        ).wait_recv()
    result = offs[0]
    for i in range(1, n):
        result = result + offs[i]
    offset[...] = result[:, :specs]

    for d in range(1, n):
        o_copy(lax.rem(me + d, n)).wait_send()
    @pl.loop(0, tiles)
    def _(t):
        for d in range(1, h):
            p = lax.rem(chip + d, h)
            g_copy(p, t).wait_send()
            forward(p, t).wait_send()
        own_core_copy(t).wait_send()
        for st in range(2):
            for j in range(per_core):
                target, copy, scale_copy = part_copy(st, j, t)

                @pl.when(target != chip)
                def _():
                    copy.wait_send()
                    scale_copy.wait_send()


def shards(coeff, weight, upper_bound, lower_depth, slopes, state, adjoint):
    boxes, specs, width = coeff.shape
    n = lax.axis_size("neuron")
    h, rows = n // 2, boxes * specs
    per_core = h // 2
    total = width * n
    tile = min(width, 512)
    tiles = width // tile
    flat = lambda v: jnp.transpose(v, (1, 0, 2)).reshape(rows, width)
    dma = lambda *s: pltpu.SemaphoreType.DMA(s)
    vmem = pl.BlockSpec(memory_space=pltpu.VMEM)
    nc, offset, slope_grad, grad = pl.pallas_call(
        functools.partial(kernel, n, boxes, specs, tile, float(total) ** -0.5),
        out_shape=(
            jax.ShapeDtypeStruct((rows, width), BF16),
            jax.ShapeDtypeStruct((boxes, specs), F32),
            jax.ShapeDtypeStruct((boxes, width), F32),
            jax.ShapeDtypeStruct((rows, width), BF16),
        ),
        in_specs=[vmem] + [pl.BlockSpec(memory_space=pltpu.HBM)] * 5 + [vmem],
        out_specs=(vmem,) * 4,
        scratch_shapes=[
            pltpu.VMEM((boxes, width), F32),
            pltpu.VMEM((boxes, width), F32),
            pltpu.VMEM((boxes, width), F32),
            pltpu.VMEM((boxes, width), jnp.int32),
            pltpu.VMEM(weight.shape, BF16),
            pltpu.VMEM((rows, width), BF16),
            pltpu.VMEM((rows, width), F32),
            pltpu.VMEM((2, per_core, rows, width), F32),
            pltpu.VMEM((2, per_core, rows, width), F32),
            pltpu.VMEM((2, per_core, rows, width), jnp.int16),
            pltpu.VMEM((2, per_core, tiles, 8, 128), F32),
            pltpu.VMEM((h, rows, width), jnp.int16),
            pltpu.VMEM((h, tiles, 8, 128), F32),
            pltpu.VMEM((2 * boxes, width), BF16),
            pltpu.VMEM((2 * boxes, width), BF16),
            pltpu.VMEM((rows, width), BF16),
            pltpu.VMEM((n, rows, width), BF16),
            pltpu.VMEM((rows, width), BF16),
            pltpu.VMEM((rows, width), BF16),
            pltpu.VMEM((-(-boxes // 16) * 16, width), BF16),
            pltpu.VMEM((2, -(-boxes // 16) * 16, width), BF16),
            pltpu.VMEM((rows, width), F32),
            pltpu.VMEM((rows, width), BF16),
            pltpu.VMEM((rows, width), BF16),
            pltpu.VMEM((rows, 128), F32),
            pltpu.VMEM((n, boxes, 128), F32),
            dma(4), dma(h * tiles), dma(2), dma(2), dma(2),
            dma(2, per_core, tiles), dma(2, per_core, tiles), dma(2, per_core, tiles),
            dma(h, tiles), dma(2, per_core, tiles), dma(h, tiles), dma(h, tiles), dma(n, tiles), dma(h, tiles),
            dma(2), dma(2), dma(2), dma(tiles), dma(tiles), dma(n), dma(n),
        ],
        compiler_params=pltpu.CompilerParams(
            collective_id=0, has_side_effects=True, vmem_limit_bytes=63 * 1024 * 1024
        ),
        cost_estimate=pl.CostEstimate(
            flops=8 * rows * weight.size, bytes_accessed=2 * weight.size, transcendentals=0
        ),
    )(
        flat(coeff), weight, upper_bound, lower_depth, slopes, state, flat(adjoint),
    )
    wide = lambda v: jnp.transpose(v.reshape(specs, boxes, width), (1, 0, 2))
    return (
        wide(nc), offset, slope_grad, wide(grad),
    )


def solution(mesh):
    return jax.shard_map(
        shards,
        mesh=mesh,
        in_specs=(
            P("box", "spec", "neuron"),
            P("neuron", "spec"),
            P("box", "neuron"),
            P("box", "neuron"),
            P("box", "neuron"),
            P("box", "neuron"),
            P("box", "spec", "neuron"),
        ),
        out_specs=(
            P("box", "spec", "neuron"),
            P("box", "spec"),
            P("box", "neuron"),
            P("box", "spec", "neuron"),
        ),
        check_vma=False,
    )
```

```python
import functools

import jax
import jax.numpy as jnp
from jax import lax
from jax.experimental import pallas as pl
from jax.experimental.pallas import tpu as pltpu
from jax.sharding import PartitionSpec as P

MESH = pl.DeviceIdType.MESH
F32 = jnp.float32
BF16 = jnp.bfloat16


def kernel(
    n, boxes, specs, tile, scale,
    coeff, weight, low, high, bound, adjoint,
    new_coeff, offset, slope_grad, coeff_grad,
    held, other, mine, theirs, crossed, coded, scales, parts, part_scales, t_adjoint, cotan,
    nc_out, nc_in, sg_sum, sg_out, sg_in, kept, away, back, off_part, offs,
    w_sem, a_sem, t_sem, c_send, c_recv, b_send, b_recv, d_send, d_recv, g_send, g_recv, f_send,
    n_sem, s_sem, e_send, e_recv, o_send, o_recv,
):
    me, sp = lax.axis_index("neuron"), lax.axis_index("spec")
    h = n // 2
    per_core = h // 2
    core, chip = lax.rem(me, 2), lax.div(me, 2)
    mate = me + 1 - 2 * core
    is_owner = lax.div(me, h) == sp
    not_owner = jnp.logical_not(is_owner)
    spot = lax.rem(me, h)
    rows, width = coeff.shape
    tiles = width // tile

    def remote(src, dst, send, recv, neuron, spec):
        return pltpu.make_async_remote_copy(
            src_ref=src, dst_ref=dst, send_sem=send, recv_sem=recv,
            device_id={"neuron": neuron, "spec": spec}, device_id_type=MESH,
        )

    def order(k):
        j = lax.rem(k, per_core)
        return 2 * j + jnp.where(k < per_core, 1 - core, core)

    def columns(q, t):
        return pl.ds(pl.multiple_of(q * width + t * tile, tile), tile)

    def load(k):
        q, t = order(lax.div(k, tiles)), lax.rem(k, tiles)
        return pltpu.make_async_copy(
            weight.at[:, columns(q, t)], held.at[:, columns(q, t)], w_sem.at[k]
        )

    @pl.loop(0, h * tiles)
    def _(k):
        load(k).start()

    barrier = pltpu.get_barrier_semaphore()
    for d in range(1, 2 * n):
        flat = lax.rem(me * 2 + sp + d, 2 * n)
        pl.semaphore_signal(
            barrier, inc=1,
            device_id={"neuron": lax.div(flat, 2), "spec": lax.rem(flat, 2)},
            device_id_type=MESH,
        )

    pl.semaphore_wait(barrier, 2 * n - 1)

    a_copy = remote(coeff, other, a_sem.at[0], a_sem.at[1], me, 1 - sp)
    a_copy.start()
    adjoint_copy = remote(adjoint, t_adjoint, t_sem.at[0], t_sem.at[1], me, 1 - sp)
    nc_copy = remote(nc_out, nc_in, n_sem.at[0], n_sem.at[1], me, 1 - sp)
    sg_copy = remote(sg_out, sg_in, s_sem.at[0], s_sem.at[1], me, 1 - sp)

    def core_copy(st, j, t):
        cols = columns(0, t)
        return remote(
            theirs.at[st, j, :, cols], crossed.at[st, j, :, cols],
            c_send.at[st, j, t], c_recv.at[st, j, t], mate, sp,
        )

    def part_copy(st, j, t):
        target = sp * per_core + j
        cols = columns(0, t)
        return target, remote(
            coded.at[st, j, :, cols], parts.at[st, chip, :, cols],
            b_send.at[st, j, t], b_recv.at[st, chip, t], target * 2 + core, sp,
        ), remote(
            scales.at[st, j, t], part_scales.at[st, chip, t],
            d_send.at[st, j, t], d_recv.at[st, chip, t], target * 2 + core, sp,
        )

    diagonal = lax.broadcasted_iota(jnp.int32, (rows, 128), 0) == lax.broadcasted_iota(
        jnp.int32, (rows, 128), 1
    )

    def block(st):
        return (sp if st == 0 else 1 - sp) * h + spot

    def g_copy(st, p, t):
        cols = columns(0, t)
        return remote(
            cotan.at[block(st), :, cols], cotan.at[block(st), :, cols],
            g_send.at[st, p, t], g_recv.at[block(st), t], p * 2 + core, sp,
        )

    def own_core_copy(st, t):
        cols = columns(0, t)
        return remote(
            cotan.at[block(st), :, cols], cotan.at[block(st), :, cols],
            g_send.at[st, chip, t], g_recv.at[block(st), t], mate, sp,
        )

    def relax(st):
        @pl.loop(0, tiles)
        def _(t):
            cols = columns(0, t)
            pre = mine[st, :, cols]
            for d in range(1, h):
                source = lax.rem(chip + d, h)
                pltpu.make_async_remote_copy(
                    src_ref=coded.at[0, 0, :, cols], dst_ref=parts.at[st, source, :, cols],
                    send_sem=b_send.at[0, 0, t], recv_sem=b_recv.at[st, source, t],
                    device_id={"neuron": mate, "spec": sp}, device_id_type=MESH,
                ).wait_recv()
                pltpu.make_async_remote_copy(
                    src_ref=scales.at[0, 0, t], dst_ref=part_scales.at[st, source, t],
                    send_sem=d_send.at[0, 0, t], recv_sem=d_recv.at[st, source, t],
                    device_id={"neuron": mate, "spec": sp}, device_id_type=MESH,
                ).wait_recv()
                step = jnp.where(diagonal, part_scales[st, source, t][:1], 0.0)
                step = jnp.sum(step, axis=1, keepdims=True)
                pre = pre + parts[st, source, :, cols].astype(jnp.int32).astype(F32) * step
            above = jnp.concatenate([low[:, cols]] * specs, axis=0)
            below = jnp.concatenate([high[:, cols]] * specs, axis=0)
            cot = (adjoint if st == 0 else t_adjoint)[:, cols].astype(F32)
            positive = jnp.maximum(pre, 0.0)
            cotan[block(st), :, cols] = (cot * jnp.where(pre > 0.0, above, below)).astype(BF16)
            for d in range(1, h):
                g_copy(st, lax.rem(chip + d, h), t).start()
            own_core_copy(st, t).start()
            relaxed = (above * positive + below * jnp.minimum(pre, 0.0)).astype(BF16)
            if st == 0:
                nc_in[:, cols] = relaxed
            else:
                nc_out[:, cols] = relaxed
            terms = cot * positive
            total = terms[:boxes]
            for s in range(1, specs):
                total = total + terms[s * boxes : (s + 1) * boxes]
            if st == 0:
                sg_sum[:, cols] = total
            else:
                total = jnp.where(bound[:, cols] > 0.0, total + sg_sum[:, cols], 0.0)
                slope_grad[:, cols] = total
                sg_out[:, cols] = jnp.concatenate(
                    [total, jnp.zeros((sg_out.shape[0] - boxes, tile), F32)], axis=0
                ).astype(BF16)

    for st in range(2):
        if st == 1:
            a_copy.wait()
        rows_in = coeff if st == 0 else other

        @pl.loop(0, per_core * tiles)
        def _(k):
            j, t = lax.div(k, tiles), lax.rem(k, tiles)
            if st == 0:
                load(k).wait()
            theirs[st, j, :, columns(0, t)] = jnp.dot(
                rows_in[...], held[:, columns(2 * j + 1 - core, t)], preferred_element_type=F32
            )
            core_copy(st, j, t).start()

        @pl.loop(0, per_core * tiles)
        def _(k):
            j, t = lax.div(k, tiles), lax.rem(k, tiles)
            cols = columns(0, t)
            if st == 0:
                load(k + per_core * tiles).wait()
            total = jnp.dot(
                rows_in[...], held[:, columns(2 * j + core, t)], preferred_element_type=F32
            )
            core_copy(st, j, t).wait()
            total = total + crossed[st, j, :, cols]
            target, copy, scale_copy = part_copy(st, j, t)

            @pl.when(target == chip)
            def _():
                mine[st, :, cols] = total

            @pl.when(target != chip)
            def _():
                largest = jnp.maximum(jnp.max(jnp.abs(total), axis=1, keepdims=True), 1e-30)
                whole = jnp.round(total * (32766.0 / largest))
                coded[st, j, :, cols] = whole.astype(jnp.int32).astype(jnp.int16)
                step = jnp.where(diagonal, largest * (1.0 / 32766.0), 0.0)
                scales[st, j, t] = jnp.broadcast_to(jnp.sum(step, axis=0, keepdims=True), (8, 128))
                copy.start()
                scale_copy.start()

        if st == 0:
            pl.when(not_owner)(adjoint_copy.start)
            pl.when(is_owner)(functools.partial(relax, 0))
        else:

            @pl.when(is_owner)
            def _():
                adjoint_copy.wait_recv()
                relax(1)
                nc_copy.start()
                sg_copy.start()

    def arrival(i, t):
        cols = columns(0, t)
        return pltpu.make_async_remote_copy(
            src_ref=cotan.at[i, :, cols], dst_ref=cotan.at[i, :, cols], send_sem=f_send.at[0, t],
            recv_sem=g_recv.at[i, t], device_id={"neuron": mate, "spec": sp},
            device_id_type=MESH,
        )

    def forward(i, t):
        cols = columns(0, t)
        return remote(
            cotan.at[i, :, cols], cotan.at[i, :, cols], f_send.at[i, t], g_recv.at[i, t], mate, sp
        )

    def e_copy(t):
        return remote(
            away.at[:, columns(0, t)], back.at[:, columns(0, t)], e_send.at[t], e_recv.at[t],
            me, 1 - sp,
        )

    def backward(spec_half):
        @pl.loop(0, tiles)
        def _(t):
            line = pl.ds(pl.multiple_of(t * tile, tile), tile)
            total = jnp.zeros((rows, tile), F32)
            for q in range(h):
                total = total + lax.dot_general(
                    cotan[spec_half * h + q], held[line, q * width : (q + 1) * width],
                    (((1,), (1,)), ((), ())), preferred_element_type=F32,
                )

            @pl.when(spec_half == sp)
            def _():
                kept[:, columns(0, t)] = total

            @pl.when(spec_half != sp)
            def _():
                away[:, columns(0, t)] = total.astype(BF16)
                e_copy(t).start()

    for spec_half in (sp, 1 - sp):
        for j in range(per_core):

            @pl.when(sp * per_core + j != chip)
            def _():
                @pl.loop(0, tiles)
                def _(t):
                    i = spec_half * h + 2 * j + core
                    arrival(i, t).wait_recv()
                    forward(i, t).start()

        @pl.loop(0, per_core * tiles)
        def _(k):
            i = spec_half * h + 2 * lax.div(k, tiles) + 1 - core
            arrival(i, lax.rem(k, tiles)).wait_recv()

        backward(spec_half)

    pl.when(not_owner)(nc_copy.wait_recv)
    off_part[...] = jnp.zeros_like(off_part)

    @pl.loop(0, tiles)
    def _(t):
        cols = columns(0, t)
        value = nc_in[:, cols]
        new_coeff[:, cols] = value
        depth = bound[:, cols] * scale
        terms = jnp.minimum(value.astype(F32), 0.0) * jnp.concatenate([depth] * specs, axis=0)
        total = terms[:, :128]
        for c in range(1, tile // 128):
            total = total + terms[:, c * 128 : (c + 1) * 128]
        off_part[...] += total

    lane = lax.broadcasted_iota(jnp.int32, (boxes, 128), 1)
    result = jnp.zeros((boxes, 128), F32)
    for k in range(specs):
        one = jnp.sum(off_part[k * boxes : (k + 1) * boxes, :], axis=1, keepdims=True)
        result = result + jnp.where(lane == k, one, 0.0)
    offs[me] = result

    def o_copy(i):
        return remote(offs.at[me], offs.at[me], o_send.at[i], o_recv.at[me], i, sp)

    for d in range(1, n):
        o_copy(lax.rem(me + d, n)).start()

    @pl.when(not_owner)
    def _():
        sg_copy.wait_recv()
        slope_grad[...] = sg_in[...].astype(F32)[:boxes]

    for t in range(tiles):
        e_copy(t).wait()
        cols = columns(0, t)
        coeff_grad[:, cols] = (kept[:, cols] + back[:, cols].astype(F32)).astype(BF16)

    for d in range(1, n):
        i = lax.rem(me + d, n)
        pltpu.make_async_remote_copy(
            src_ref=offs.at[i], dst_ref=offs.at[i], send_sem=o_send.at[me],
            recv_sem=o_recv.at[i], device_id={"neuron": mate, "spec": sp}, device_id_type=MESH,
        ).wait_recv()
    result = offs[0]
    for i in range(1, n):
        result = result + offs[i]
    offset[...] = result[:, :specs]

    for d in range(1, n):
        o_copy(lax.rem(me + d, n)).wait_send()
    @pl.when(is_owner)
    def _():
        nc_copy.wait_send()
        sg_copy.wait_send()

    pl.when(not_owner)(adjoint_copy.wait_send)

    @pl.loop(0, tiles)
    def _(t):
        @pl.when(is_owner)
        def _():
            for st in range(2):
                for d in range(1, h):
                    g_copy(st, lax.rem(chip + d, h), t).wait_send()
                own_core_copy(st, t).wait_send()

        for j in range(per_core):

            @pl.when(sp * per_core + j != chip)
            def _():
                for st in range(2):
                    _, copy, scale_copy = part_copy(st, j, t)
                    copy.wait_send()
                    scale_copy.wait_send()
                    forward(st * h + 2 * j + core, t).wait_send()


def shards(coeff, weight, upper_bound, lower_depth, slopes, state, adjoint):
    boxes, specs, width = coeff.shape
    n = lax.axis_size("neuron")
    h, rows = n // 2, boxes * specs
    per_core = h // 2
    total = width * n
    tile = min(width, 512)
    tiles = width // tile
    flat = lambda v: jnp.transpose(v, (1, 0, 2)).reshape(rows, width)
    dma = lambda *s: pltpu.SemaphoreType.DMA(s)
    vmem = pl.BlockSpec(memory_space=pltpu.VMEM)
    unstable = state == 2
    solid = jnp.where(state == 1, 1.0, 0.0)
    low = jnp.where(unstable, slopes, solid)
    high = jnp.where(unstable, upper_bound / (upper_bound + lower_depth), solid)
    bound = jnp.where(unstable, lower_depth, 0.0)
    nc, offset, slope_grad, grad = pl.pallas_call(
        functools.partial(kernel, n, boxes, specs, tile, float(total) ** -0.5),
        out_shape=(
            jax.ShapeDtypeStruct((rows, width), BF16),
            jax.ShapeDtypeStruct((boxes, specs), F32),
            jax.ShapeDtypeStruct((boxes, width), F32),
            jax.ShapeDtypeStruct((rows, width), BF16),
        ),
        in_specs=[vmem, pl.BlockSpec(memory_space=pltpu.HBM)] + [vmem] * 4,
        out_specs=(vmem,) * 4,
        scratch_shapes=[
            pltpu.VMEM(weight.shape, BF16),
            pltpu.VMEM((rows, width), BF16),
            pltpu.VMEM((2, rows, width), F32),
            pltpu.VMEM((2, per_core, rows, width), F32),
            pltpu.VMEM((2, per_core, rows, width), F32),
            pltpu.VMEM((2, per_core, rows, width), jnp.int16),
            pltpu.VMEM((2, per_core, tiles, 8, 128), F32),
            pltpu.VMEM((2, h, rows, width), jnp.int16),
            pltpu.VMEM((2, h, tiles, 8, 128), F32),
            pltpu.VMEM((rows, width), BF16),
            pltpu.VMEM((n, rows, width), BF16),
            pltpu.VMEM((rows, width), BF16),
            pltpu.VMEM((rows, width), BF16),
            pltpu.VMEM((boxes, width), F32),
            pltpu.VMEM((-(-boxes // 16) * 16, width), BF16),
            pltpu.VMEM((-(-boxes // 16) * 16, width), BF16),
            pltpu.VMEM((rows, width), F32),
            pltpu.VMEM((rows, width), BF16),
            pltpu.VMEM((rows, width), BF16),
            pltpu.VMEM((rows, 128), F32),
            pltpu.VMEM((n, boxes, 128), F32),
            dma(h * tiles), dma(2), dma(2),
            dma(2, per_core, tiles), dma(2, per_core, tiles), dma(2, per_core, tiles),
            dma(2, h, tiles), dma(2, per_core, tiles), dma(2, h, tiles),
            dma(2, h, tiles), dma(n, tiles), dma(n, tiles),
            dma(2), dma(2), dma(tiles), dma(tiles), dma(n), dma(n),
        ],
        compiler_params=pltpu.CompilerParams(
            collective_id=0, has_side_effects=True, vmem_limit_bytes=48 * 1024 * 1024
        ),
        cost_estimate=pl.CostEstimate(
            flops=8 * rows * weight.size, bytes_accessed=2 * weight.size, transcendentals=0
        ),
    )(
        flat(coeff), weight, low, high, bound, flat(adjoint),
    )
    wide = lambda v: jnp.transpose(v.reshape(specs, boxes, width), (1, 0, 2))
    return (
        wide(nc), offset, slope_grad, wide(grad),
    )


def solution(mesh):
    return jax.shard_map(
        shards,
        mesh=mesh,
        in_specs=(
            P("box", "spec", "neuron"),
            P("neuron", "spec"),
            P("box", "neuron"),
            P("box", "neuron"),
            P("box", "neuron"),
            P("box", "neuron"),
            P("box", "spec", "neuron"),
        ),
        out_specs=(
            P("box", "spec", "neuron"),
            P("box", "spec"),
            P("box", "neuron"),
            P("box", "spec", "neuron"),
        ),
        check_vma=False,
    )
```

```python
import functools

import jax
import jax.numpy as jnp
from jax import lax
from jax.experimental import pallas as pl
from jax.experimental.pallas import tpu as pltpu
from jax.sharding import PartitionSpec as P

MESH = pl.DeviceIdType.MESH
F32 = jnp.float32
BF16 = jnp.bfloat16


def kernel(
    n, boxes, specs, tile, scale,
    coeff, weight, low, high, bound, adjoint,
    new_coeff, offset, slope_grad, coeff_grad,
    held, other, mine, theirs, crossed, coded, scales, parts, part_scales, t_adjoint, cotan,
    nc_out, nc_in, sg_sum, sg_out, sg_in, kept, away, back, off_part, offs,
    w_sem, a_sem, t_sem, c_send, c_recv, b_send, b_recv, d_send, d_recv, g_send, g_recv, f_send,
    n_sem, s_sem, e_send, e_recv, o_send, o_recv,
):
    me, sp = lax.axis_index("neuron"), lax.axis_index("spec")
    h = n // 2
    per_core = h // 2
    core, chip = lax.rem(me, 2), lax.div(me, 2)
    mate = me + 1 - 2 * core
    is_owner = lax.div(me, h) == sp
    not_owner = jnp.logical_not(is_owner)
    spot = lax.rem(me, h)
    rows, width = coeff.shape
    tiles = width // tile

    def remote(src, dst, send, recv, neuron, spec):
        return pltpu.make_async_remote_copy(
            src_ref=src, dst_ref=dst, send_sem=send, recv_sem=recv,
            device_id={"neuron": neuron, "spec": spec}, device_id_type=MESH,
        )

    def columns(q, t):
        return pl.ds(pl.multiple_of(q * width + t * tile, tile), tile)

    def load(k):
        pair = lax.div(k, 2)
        j, t = lax.div(pair, tiles), lax.rem(pair, tiles)
        q = 2 * j + jnp.where(lax.rem(k, 2) == 0, 1 - core, core)
        return pltpu.make_async_copy(
            weight.at[:, columns(q, t)], held.at[:, columns(q, t)], w_sem.at[k]
        )

    @pl.loop(0, h * tiles)
    def _(k):
        load(k).start()

    barrier = pltpu.get_barrier_semaphore()
    for d in range(1, 2 * n):
        flat = lax.rem(me * 2 + sp + d, 2 * n)
        pl.semaphore_signal(
            barrier, inc=1,
            device_id={"neuron": lax.div(flat, 2), "spec": lax.rem(flat, 2)},
            device_id_type=MESH,
        )

    pl.semaphore_wait(barrier, 2 * n - 1)

    a_copy = remote(coeff, other, a_sem.at[0], a_sem.at[1], me, 1 - sp)
    a_copy.start()
    adjoint_copy = remote(adjoint, t_adjoint, t_sem.at[0], t_sem.at[1], me, 1 - sp)
    nc_copy = remote(nc_out, nc_in, n_sem.at[0], n_sem.at[1], me, 1 - sp)
    sg_copy = remote(sg_out, sg_in, s_sem.at[0], s_sem.at[1], me, 1 - sp)

    def core_copy(st, j, t):
        cols = columns(0, t)
        return remote(
            theirs.at[st, j, :, cols], crossed.at[st, j, :, cols],
            c_send.at[st, j, t], c_recv.at[st, j, t], mate, sp,
        )

    def part_copy(st, j, t):
        target = sp * per_core + j
        cols = columns(0, t)
        return target, remote(
            coded.at[st, j, :, cols], parts.at[st, chip, :, cols],
            b_send.at[st, j, t], b_recv.at[st, chip, t], target * 2 + core, sp,
        ), remote(
            scales.at[st, j, t], part_scales.at[st, chip, t],
            d_send.at[st, j, t], d_recv.at[st, chip, t], target * 2 + core, sp,
        )

    diagonal = lax.broadcasted_iota(jnp.int32, (rows, 128), 0) == lax.broadcasted_iota(
        jnp.int32, (rows, 128), 1
    )

    def block(st):
        return (sp if st == 0 else 1 - sp) * h + spot

    def g_copy(st, p, t):
        cols = columns(0, t)
        return remote(
            cotan.at[block(st), :, cols], cotan.at[block(st), :, cols],
            g_send.at[st, p, t], g_recv.at[block(st), t], p * 2 + core, sp,
        )

    def own_core_copy(st, t):
        cols = columns(0, t)
        return remote(
            cotan.at[block(st), :, cols], cotan.at[block(st), :, cols],
            g_send.at[st, chip, t], g_recv.at[block(st), t], mate, sp,
        )

    def relax(st):
        @pl.loop(0, tiles)
        def _(t):
            cols = columns(0, t)
            pre = mine[st, :, cols]
            for d in range(1, h):
                source = lax.rem(chip + d, h)
                pltpu.make_async_remote_copy(
                    src_ref=coded.at[0, 0, :, cols], dst_ref=parts.at[st, source, :, cols],
                    send_sem=b_send.at[0, 0, t], recv_sem=b_recv.at[st, source, t],
                    device_id={"neuron": mate, "spec": sp}, device_id_type=MESH,
                ).wait_recv()
                pltpu.make_async_remote_copy(
                    src_ref=scales.at[0, 0, t], dst_ref=part_scales.at[st, source, t],
                    send_sem=d_send.at[0, 0, t], recv_sem=d_recv.at[st, source, t],
                    device_id={"neuron": mate, "spec": sp}, device_id_type=MESH,
                ).wait_recv()
                step = jnp.where(diagonal, part_scales[st, source, t][:1], 0.0)
                step = jnp.sum(step, axis=1, keepdims=True)
                pre = pre + parts[st, source, :, cols].astype(jnp.int32).astype(F32) * step
            above = jnp.concatenate([low[:, cols]] * specs, axis=0)
            below = jnp.concatenate([high[:, cols]] * specs, axis=0)
            cot = (adjoint if st == 0 else t_adjoint)[:, cols].astype(F32)
            positive = jnp.maximum(pre, 0.0)
            cotan[block(st), :, cols] = (cot * jnp.where(pre > 0.0, above, below)).astype(BF16)
            for d in range(1, h):
                g_copy(st, lax.rem(chip + d, h), t).start()
            own_core_copy(st, t).start()
            relaxed = (above * positive + below * jnp.minimum(pre, 0.0)).astype(BF16)
            if st == 0:
                nc_in[:, cols] = relaxed
            else:
                nc_out[:, cols] = relaxed
            terms = cot * positive
            total = terms[:boxes]
            for s in range(1, specs):
                total = total + terms[s * boxes : (s + 1) * boxes]
            if st == 0:
                sg_sum[:, cols] = total
            else:
                total = jnp.where(bound[:, cols] > 0.0, total + sg_sum[:, cols], 0.0)
                slope_grad[:, cols] = total
                sg_out[:, cols] = jnp.concatenate(
                    [total, jnp.zeros((sg_out.shape[0] - boxes, tile), F32)], axis=0
                ).astype(BF16)

    for st in range(2):
        if st == 1:
            a_copy.wait()
        rows_in = coeff if st == 0 else other

        def give(k):
            j, t = lax.div(k, tiles), lax.rem(k, tiles)
            if st == 0:
                load(2 * k).wait()
            theirs[st, j, :, columns(0, t)] = jnp.dot(
                rows_in[...], held[:, columns(2 * j + 1 - core, t)], preferred_element_type=F32
            )
            core_copy(st, j, t).start()

        def take(k):
            j, t = lax.div(k, tiles), lax.rem(k, tiles)
            cols = columns(0, t)
            if st == 0:
                load(2 * k + 1).wait()
            total = jnp.dot(
                rows_in[...], held[:, columns(2 * j + core, t)], preferred_element_type=F32
            )
            core_copy(st, j, t).wait()
            total = total + crossed[st, j, :, cols]
            target, copy, scale_copy = part_copy(st, j, t)

            @pl.when(target == chip)
            def _():
                mine[st, :, cols] = total

            @pl.when(target != chip)
            def _():
                largest = jnp.maximum(jnp.max(jnp.abs(total), axis=1, keepdims=True), 1e-30)
                whole = jnp.round(total * (32766.0 / largest))
                coded[st, j, :, cols] = whole.astype(jnp.int32).astype(jnp.int16)
                step = jnp.where(diagonal, largest * (1.0 / 32766.0), 0.0)
                scales[st, j, t] = jnp.broadcast_to(jnp.sum(step, axis=0, keepdims=True), (8, 128))
                copy.start()
                scale_copy.start()

        give(0)

        @pl.loop(1, per_core * tiles)
        def _(k):
            give(k)
            take(k - 1)

        take(per_core * tiles - 1)

        if st == 0:
            pl.when(not_owner)(adjoint_copy.start)
            pl.when(is_owner)(functools.partial(relax, 0))
        else:

            @pl.when(is_owner)
            def _():
                adjoint_copy.wait_recv()
                relax(1)
                nc_copy.start()
                sg_copy.start()

    def arrival(i, t):
        cols = columns(0, t)
        return pltpu.make_async_remote_copy(
            src_ref=cotan.at[i, :, cols], dst_ref=cotan.at[i, :, cols], send_sem=f_send.at[0, t],
            recv_sem=g_recv.at[i, t], device_id={"neuron": mate, "spec": sp},
            device_id_type=MESH,
        )

    def forward(i, t):
        cols = columns(0, t)
        return remote(
            cotan.at[i, :, cols], cotan.at[i, :, cols], f_send.at[i, t], g_recv.at[i, t], mate, sp
        )

    def e_copy(t):
        return remote(
            away.at[:, columns(0, t)], back.at[:, columns(0, t)], e_send.at[t], e_recv.at[t],
            me, 1 - sp,
        )

    def backward(spec_half):
        @pl.loop(0, tiles)
        def _(t):
            line = pl.ds(pl.multiple_of(t * tile, tile), tile)
            total = jnp.zeros((rows, tile), F32)
            for q in range(h):
                total = total + lax.dot_general(
                    cotan[spec_half * h + q], held[line, q * width : (q + 1) * width],
                    (((1,), (1,)), ((), ())), preferred_element_type=F32,
                )

            @pl.when(spec_half == sp)
            def _():
                kept[:, columns(0, t)] = total

            @pl.when(spec_half != sp)
            def _():
                away[:, columns(0, t)] = total.astype(BF16)
                e_copy(t).start()

    for spec_half in (sp, 1 - sp):
        for j in range(per_core):

            @pl.when(sp * per_core + j != chip)
            def _():
                @pl.loop(0, tiles)
                def _(t):
                    i = spec_half * h + 2 * j + core
                    arrival(i, t).wait_recv()
                    forward(i, t).start()

        @pl.loop(0, per_core * tiles)
        def _(k):
            i = spec_half * h + 2 * lax.div(k, tiles) + 1 - core
            arrival(i, lax.rem(k, tiles)).wait_recv()

        backward(spec_half)

    pl.when(not_owner)(nc_copy.wait_recv)
    off_part[...] = jnp.zeros_like(off_part)

    @pl.loop(0, tiles)
    def _(t):
        cols = columns(0, t)
        value = nc_in[:, cols]
        new_coeff[:, cols] = value
        depth = bound[:, cols] * scale
        terms = jnp.minimum(value.astype(F32), 0.0) * jnp.concatenate([depth] * specs, axis=0)
        total = terms[:, :128]
        for c in range(1, tile // 128):
            total = total + terms[:, c * 128 : (c + 1) * 128]
        off_part[...] += total

    lane = lax.broadcasted_iota(jnp.int32, (boxes, 128), 1)
    result = jnp.zeros((boxes, 128), F32)
    for k in range(specs):
        one = jnp.sum(off_part[k * boxes : (k + 1) * boxes, :], axis=1, keepdims=True)
        result = result + jnp.where(lane == k, one, 0.0)
    offs[me] = result

    def o_copy(i):
        return remote(offs.at[me], offs.at[me], o_send.at[i], o_recv.at[me], i, sp)

    for d in range(1, n):
        o_copy(lax.rem(me + d, n)).start()

    @pl.when(not_owner)
    def _():
        sg_copy.wait_recv()
        slope_grad[...] = sg_in[...].astype(F32)[:boxes]

    for t in range(tiles):
        e_copy(t).wait()
        cols = columns(0, t)
        coeff_grad[:, cols] = (kept[:, cols] + back[:, cols].astype(F32)).astype(BF16)

    for d in range(1, n):
        i = lax.rem(me + d, n)
        pltpu.make_async_remote_copy(
            src_ref=offs.at[i], dst_ref=offs.at[i], send_sem=o_send.at[me],
            recv_sem=o_recv.at[i], device_id={"neuron": mate, "spec": sp}, device_id_type=MESH,
        ).wait_recv()
    result = offs[0]
    for i in range(1, n):
        result = result + offs[i]
    offset[...] = result[:, :specs]

    for d in range(1, n):
        o_copy(lax.rem(me + d, n)).wait_send()
    @pl.when(is_owner)
    def _():
        nc_copy.wait_send()
        sg_copy.wait_send()

    pl.when(not_owner)(adjoint_copy.wait_send)

    @pl.loop(0, tiles)
    def _(t):
        @pl.when(is_owner)
        def _():
            for st in range(2):
                for d in range(1, h):
                    g_copy(st, lax.rem(chip + d, h), t).wait_send()
                own_core_copy(st, t).wait_send()

        for j in range(per_core):

            @pl.when(sp * per_core + j != chip)
            def _():
                for st in range(2):
                    _, copy, scale_copy = part_copy(st, j, t)
                    copy.wait_send()
                    scale_copy.wait_send()
                    forward(st * h + 2 * j + core, t).wait_send()


def shards(coeff, weight, upper_bound, lower_depth, slopes, state, adjoint):
    boxes, specs, width = coeff.shape
    n = lax.axis_size("neuron")
    h, rows = n // 2, boxes * specs
    per_core = h // 2
    total = width * n
    tile = min(width, 512)
    tiles = width // tile
    flat = lambda v: jnp.transpose(v, (1, 0, 2)).reshape(rows, width)
    dma = lambda *s: pltpu.SemaphoreType.DMA(s)
    vmem = pl.BlockSpec(memory_space=pltpu.VMEM)
    unstable = state == 2
    solid = jnp.where(state == 1, 1.0, 0.0)
    low = jnp.where(unstable, slopes, solid)
    high = jnp.where(unstable, upper_bound / (upper_bound + lower_depth), solid)
    bound = jnp.where(unstable, lower_depth, 0.0)
    nc, offset, slope_grad, grad = pl.pallas_call(
        functools.partial(kernel, n, boxes, specs, tile, float(total) ** -0.5),
        out_shape=(
            jax.ShapeDtypeStruct((rows, width), BF16),
            jax.ShapeDtypeStruct((boxes, specs), F32),
            jax.ShapeDtypeStruct((boxes, width), F32),
            jax.ShapeDtypeStruct((rows, width), BF16),
        ),
        in_specs=[vmem, pl.BlockSpec(memory_space=pltpu.HBM)] + [vmem] * 4,
        out_specs=(vmem,) * 4,
        scratch_shapes=[
            pltpu.VMEM(weight.shape, BF16),
            pltpu.VMEM((rows, width), BF16),
            pltpu.VMEM((2, rows, width), F32),
            pltpu.VMEM((2, per_core, rows, width), F32),
            pltpu.VMEM((2, per_core, rows, width), F32),
            pltpu.VMEM((2, per_core, rows, width), jnp.int16),
            pltpu.VMEM((2, per_core, tiles, 8, 128), F32),
            pltpu.VMEM((2, h, rows, width), jnp.int16),
            pltpu.VMEM((2, h, tiles, 8, 128), F32),
            pltpu.VMEM((rows, width), BF16),
            pltpu.VMEM((n, rows, width), BF16),
            pltpu.VMEM((rows, width), BF16),
            pltpu.VMEM((rows, width), BF16),
            pltpu.VMEM((boxes, width), F32),
            pltpu.VMEM((-(-boxes // 16) * 16, width), BF16),
            pltpu.VMEM((-(-boxes // 16) * 16, width), BF16),
            pltpu.VMEM((rows, width), F32),
            pltpu.VMEM((rows, width), BF16),
            pltpu.VMEM((rows, width), BF16),
            pltpu.VMEM((rows, 128), F32),
            pltpu.VMEM((n, boxes, 128), F32),
            dma(h * tiles), dma(2), dma(2),
            dma(2, per_core, tiles), dma(2, per_core, tiles), dma(2, per_core, tiles),
            dma(2, h, tiles), dma(2, per_core, tiles), dma(2, h, tiles),
            dma(2, h, tiles), dma(n, tiles), dma(n, tiles),
            dma(2), dma(2), dma(tiles), dma(tiles), dma(n), dma(n),
        ],
        compiler_params=pltpu.CompilerParams(
            collective_id=0, has_side_effects=True, vmem_limit_bytes=48 * 1024 * 1024
        ),
        cost_estimate=pl.CostEstimate(
            flops=8 * rows * weight.size, bytes_accessed=2 * weight.size, transcendentals=0
        ),
    )(
        flat(coeff), weight, low, high, bound, flat(adjoint),
    )
    wide = lambda v: jnp.transpose(v.reshape(specs, boxes, width), (1, 0, 2))
    return (
        wide(nc), offset, slope_grad, wide(grad),
    )


def solution(mesh):
    return jax.shard_map(
        shards,
        mesh=mesh,
        in_specs=(
            P("box", "spec", "neuron"),
            P("neuron", "spec"),
            P("box", "neuron"),
            P("box", "neuron"),
            P("box", "neuron"),
            P("box", "neuron"),
            P("box", "spec", "neuron"),
        ),
        out_specs=(
            P("box", "spec", "neuron"),
            P("box", "spec"),
            P("box", "neuron"),
            P("box", "spec", "neuron"),
        ),
        check_vma=False,
    )
```
